32 devices in a mesh: row: 4 (over y, x), col: 8 (over z, core).
Axes of the slice: x: 2, y: 2, z: 4, core: 2. Of those that a mesh axis runs over, the one named last changes fastest.
Arguments:
- matrix: float32 [8, 1024, 4, 2048], P(None, 'row', None, 'col'), may hold values from -8 to 8, as said below
Outputs:
- reduced: float32 [8, 1024, 4, 2048], P(None, 'row', None, 'col')
The draws below stay inside these ranges and needn't reach their ends.
Inputs may be any that keep to these rules, and one draw needn't show every extreme that they name: symmetric: the entries at (r, c) and (c, r) of the 8192 x 8192 matrix are equal.
All inputs are finite; a program needn't handle non-finite values.
Results may differ from the reference program's by a relative error of at most 0.0002.
Values sent between devices are 32-bit elements; how exact they have to be, the bound alone decides.
A program may use at most 128 MiB of HBM per device.

```python
import jax
import jax.numpy as jnp
from jax import lax

N = 8192
NB = 256
PANELS = 2
KR = 8
KC = 4
N_ROW = 4
N_COL = 8


def draw_matrix(key, part):
    base = jax.random.normal(jax.random.fold_in(key, 11), (N, N), jnp.float32)
    sym = (base + base.T) * 0.5
    sym = jnp.clip(sym, -8.0, 8.0)
    heavy = jax.random.uniform(jax.random.fold_in(key, 13), (NB, NB), jnp.float32, -8.0, 8.0)
    sym = sym.at[NB:2 * NB, 0:NB].set(heavy)
    sym = sym.at[0:NB, NB:2 * NB].set(heavy.T)
    return sym.reshape(KR, N_ROW * NB, KC, N_COL * NB)


def setup_inputs(seed: int = 0) -> dict:
    keys = jax.random.split(jax.random.key(seed), 2)
    return {
        "matrix": draw_matrix(jax.random.fold_in(keys[1], 71), 0),
    }


highest = lax.Precision.HIGHEST

def matmul(left, right):
    return jnp.dot(left.astype(jnp.float32), right.astype(jnp.float32), precision=highest, preferred_element_type=jnp.float32)

def reference(matrix):
    order = matrix.shape[0] * matrix.shape[1]
    dense = matrix.reshape(order, order)
    for panel in range(PANELS):
        first = panel * NB
        start = first + NB
        strip = dense[start:, first:start]
        factor = jnp.linalg.cholesky(matmul(strip.T, strip))
        basis = jax.scipy.linalg.solve_triangular(factor, strip.T, lower=True).T
        shifted = jnp.eye(NB, dtype=jnp.float32) + basis[:NB]
        normal = matmul(shifted.T, shifted)
        coupling = jax.scipy.linalg.cho_solve((jnp.linalg.cholesky(normal), True), shifted.T)
        vectors = basis.at[:NB].add(jnp.eye(NB, dtype=jnp.float32))
        trailing = dense[start:, start:]
        applied = matmul(trailing, vectors)
        middle = matmul(matmul(coupling, matmul(vectors.T, applied)), coupling.T)
        factor_y = matmul(applied, coupling.T) - 0.5 * matmul(vectors, middle)
        trailing = trailing - matmul(factor_y, vectors.T) - matmul(vectors, factor_y.T)
        block = jnp.zeros_like(strip).at[:NB].set(-factor.T)
        dense = dense.at[start:, start:].set(trailing)
        dense = dense.at[start:, first:start].set(block)
        dense = dense.at[first:start, start:].set(block.T)
    return dense.reshape(matrix.shape)
```

```python
import functools

import jax
import jax.numpy as jnp
from jax import lax
from jax.experimental import pallas as pl
from jax.experimental.pallas import tpu as pltpu
from jax.sharding import PartitionSpec as P

PANELS = 2
MESH = pl.DeviceIdType.MESH
VMEM = pl.BlockSpec(memory_space=pltpu.VMEM)
highest = lax.Precision.HIGHEST
high = lax.Precision.HIGH


def dot(left, right, precision=highest):
    return jnp.dot(left, right, precision=precision, preferred_element_type=jnp.float32)


def dot_tn(left, right):
    return lax.dot_general(left, right, (((0,), (0,)), ((), ())), precision=highest,
                           preferred_element_type=jnp.float32)


def dot_nt(left, right):
    return lax.dot_general(left, right, (((1,), (1,)), ((), ())), precision=highest,
                           preferred_element_type=jnp.float32)


def remote(src, dst, send, recv, row, col):
    return pltpu.make_async_remote_copy(src_ref=src, dst_ref=dst, send_sem=send, recv_sem=recv,
                                        device_id=(row, col), device_id_type=MESH)


def greet(devices):
    barrier = pltpu.get_barrier_semaphore()
    for cond, row, col in devices:
        def hail(row=row, col=col):
            pl.semaphore_signal(barrier, inc=1, device_id=(row, col), device_id_type=MESH)
        if cond is True:
            hail()
        else:
            pl.when(cond)(hail)
    heard = sum(1 if cond is True else cond.astype(jnp.int32) for cond, _, _ in devices)
    pl.semaphore_wait(barrier, heard)


def ring_place(row, rows):
    return row + (row // 2) * (5 - 2 * row) if rows == 4 else row


RING_CHUNKS = 4


def spread_kernel(panel, rows, cols, xr_in, xct_in, gram_in, top_in, xr, xct, gt, slots,
                  send_z, send_k, recv_z, send_a, recv_a, send_b, recv_b,
                  send_g, recv_g, send_t, recv_t):
    width = gram_in.shape[0]
    r, c = lax.axis_index("row"), lax.axis_index("col")
    z, k, chips = c // 2, c % 2, cols // 2
    root_row, root_col, top_row = panel % rows, panel % cols, (panel + 1) % rows
    core = root_col % 2
    assert root_col // 2 == 0
    blocks = xr.shape[0] // width
    place = ring_place(r, rows)
    after = ring_place((place + 1) % rows, rows)
    before = ring_place((place + rows - 1) % rows, rows)
    ahead = (place - ring_place(root_row, rows) + rows) % rows
    behind = (rows - ahead) % rows
    peers = [(r + i) % rows for i in range(1, rows)]
    greet([(True, peer, c) for peer in peers]
          + [(True, r, c + 1 - 2 * k), (z > 0, r, c - 2), (z < chips - 1, r, c + 2)])

    owner = c == root_col
    relay = k == core

    def z_piece(i):
        if i < blocks:
            return xr.at[pl.ds(i * width, width)]
        return gt.at[i - blocks]

    def to_chip(i):
        return remote(z_piece(i), z_piece(i), send_z.at[i], recv_z.at[i], r, c + 2)

    def to_core(i):
        return remote(z_piece(i), z_piece(i), send_k.at[i], recv_z.at[i], r, c + 1 - 2 * k)

    def forward(i):
        pl.when(z < chips - 1)(lambda: to_chip(i).start())
        to_core(i).start()

    def gram_to(i, peer):
        return remote(gram_in, slots.at[i - 1], send_g.at[i - 1], recv_g.at[i - 1], peer, c)

    def top_to(i, peer):
        return remote(gt.at[1], gt.at[1], send_t.at[i - 1], recv_t, peer, c)

    half = width // 2
    step = half // RING_CHUNKS

    def ring_piece(side, i):
        return xct.at[pl.ds(side * half + i * step, step)]

    def to_after(i):
        return remote(ring_piece(0, i), ring_piece(0, i), send_a.at[i], recv_a.at[i], after, c)

    def to_before(i):
        return remote(ring_piece(1, i), ring_piece(1, i), send_b.at[i], recv_b.at[i], before, c)

    @pl.when(owner)
    def _():
        for i, peer in enumerate(peers, 1):
            gram_to(i, peer).start()

        @pl.when(r == top_row)
        def _():
            gt[1] = top_in[...]
            for i, peer in enumerate(peers, 1):
                top_to(i, peer).start()

    @pl.when(ahead == 0)
    def _():
        xct[...] = xct_in[...]
        for i in range(RING_CHUNKS):
            to_after(i).start()
            to_before(i).start()

    @pl.when(owner)
    def _():
        for i in range(blocks):
            xr[pl.ds(i * width, width), :] = xr_in[pl.ds(i * width, width), :]
            forward(i)
        total = gram_in[...]
        for i, peer in enumerate(peers, 1):
            gram_to(i, peer).wait()
            total = total + slots[i - 1]
        gt[0] = total
        forward(blocks)

        @pl.when(r != top_row)
        def _():
            top_to(1, peers[0]).wait_recv()

        forward(blocks + 1)

    for i in range(max(blocks + 2, RING_CHUNKS)):
        if i < RING_CHUNKS:
            @pl.when(ahead != 0)
            def _(i=i):
                to_after(i).wait_recv()
                pl.when(ahead < rows - 1)(lambda: to_after(i).start())
                to_before(i).wait_recv()
                pl.when(behind < rows - 1)(lambda: to_before(i).start())
        if i < blocks + 2:
            @pl.when(jnp.logical_not(owner))
            def _(i=i):
                to_core(i).wait_recv()
                pl.when(relay)(lambda: forward(i))

    @pl.when(owner & (r == top_row))
    def _():
        for i, peer in enumerate(peers, 1):
            top_to(i, peer).wait_send()

    @pl.when(relay)
    def _():
        for i in range(blocks + 2):
            pl.when(z < chips - 1)(lambda: to_chip(i).wait_send())
            to_core(i).wait_send()

    for i in range(RING_CHUNKS):
        pl.when(ahead < rows - 1)(lambda: to_after(i).wait_send())
        pl.when(behind < rows - 1)(lambda: to_before(i).wait_send())


def spread(panel, rows, cols, xr, xct, gram, top):
    width = gram.shape[0]
    pieces = xr.shape[0] // width + 2
    dma = pltpu.SemaphoreType.DMA
    f32 = jnp.float32
    return pl.pallas_call(
        functools.partial(spread_kernel, panel, rows, cols),
        out_shape=(jax.ShapeDtypeStruct(xr.shape, f32), jax.ShapeDtypeStruct(xct.shape, f32),
                   jax.ShapeDtypeStruct((2, width, width), f32)),
        in_specs=[VMEM] * 4,
        out_specs=(VMEM,) * 3,
        scratch_shapes=[pltpu.VMEM((rows - 1, width, width), f32),
                        dma((pieces,)), dma((pieces,)), dma((pieces,)),
                        dma((RING_CHUNKS,)), dma((RING_CHUNKS,)), dma((RING_CHUNKS,)), dma((RING_CHUNKS,)),
                        dma((rows - 1,)), dma((rows - 1,)), dma((rows - 1,)), dma],
        compiler_params=pltpu.CompilerParams(collective_id=panel, has_side_effects=True,
                                             vmem_limit_bytes=40 * 2**20),
        name=f"spread_panel_{panel}",
    )(xr, xct, gram, top)


GROUP = 4


def eliminate(block):
    size = block.shape[0]
    row = lax.broadcasted_iota(jnp.int32, (size, size), 0)
    col = lax.broadcasted_iota(jnp.int32, (size, size), 1)
    eye = (row == col).astype(jnp.float32)
    work = jnp.concatenate([block, eye], axis=1)
    lane_rows = lax.broadcasted_iota(jnp.int32, work.shape, 0)
    for base in range(0, size, GROUP):
        columns = [jnp.broadcast_to(work[:, base + i:base + i + 1], work.shape) for i in range(GROUP)]
        pivots = [work[base + i:base + i + 1, :] for i in range(GROUP)]
        change = None
        for i in range(GROUP):
            at = base + i
            inverse = 1.0 / columns[i][at:at + 1, :]
            factor = jnp.where(lane_rows > at, columns[i] * inverse, 0.0)
            for l in range(i + 1, GROUP):
                columns[l] = columns[l] - factor * columns[l][at:at + 1, :]
                pivots[l] = pivots[l] - factor[base + l:base + l + 1, :] * pivots[i]
            term = factor * pivots[i]
            change = term if change is None else change + term
        work = work - change
    diagonal = jnp.sum(jnp.where(row == col, work[:, :size], 0.0), axis=1, keepdims=True)
    return jnp.where(row >= col, work[:, size:] * lax.rsqrt(diagonal), 0.0)


def factorize(work, size):
    width = work.shape[0]
    for start in range(0, width, size):
        stop = start + size
        inverse = eliminate(work[start:stop, start:stop])
        strip = dot(inverse, work[start:stop, :])
        work[start:stop, :] = strip
        if stop < width:
            work[stop:, :] = work[stop:, :] - dot_tn(strip[:, stop:width], strip)


def factor_kernel(gt, upper, lower_inverse, coupling, work):
    width = upper.shape[0]
    row = lax.broadcasted_iota(jnp.int32, (width, width), 0)
    col = lax.broadcasted_iota(jnp.int32, (width, width), 1)
    eye = (row == col).astype(jnp.float32)
    work[:, :width] = gt[0]
    work[:, width:] = eye
    factorize(work, 64)
    upper[...] = jnp.where(row <= col, work[:, :width], 0.0)
    inverse = work[:, width:]
    lower_inverse[...] = inverse
    shifted = eye + dot_nt(gt[1], inverse)
    work[:, :width] = dot_tn(shifted, shifted)
    work[:, width:] = eye
    factorize(work, 64)
    inverse = work[:, width:]
    coupling[...] = dot_tn(inverse, dot_nt(inverse, shifted))


def factors(panel, gt):
    width = gt.shape[1]
    square = jax.ShapeDtypeStruct((width, width), jnp.float32)
    return pl.pallas_call(
        factor_kernel,
        out_shape=(square,) * 3,
        in_specs=[VMEM],
        out_specs=(VMEM,) * 3,
        scratch_shapes=[pltpu.VMEM((width, 2 * width), jnp.float32)],
        compiler_params=pltpu.CompilerParams(vmem_limit_bytes=32 * 2**20),
        name=f"factors_{panel}",
    )(gt)


def product_kernel(rows, cols, part, wct, wrt, slots, send_s, recv_s, send_g, recv_g,
                   send_up, send_down, send_k, recv_z):
    r, c = lax.axis_index("row"), lax.axis_index("col")
    z, k, chips = c // 2, c % 2, cols // 2
    share = part.shape[0] // rows
    halves = cols // rows
    relay = k == r % 2
    peers = [(r + i) % rows for i in range(1, rows)]
    greet([(True, peer, c) for peer in peers]
          + [(True, r, c + 1 - 2 * k), (z > 0, r, c - 2), (z < chips - 1, r, c + 2)])

    def rows_of(q):
        return pl.ds(pl.multiple_of(q * share, share), share)

    def scatter(i):
        return remote(part.at[rows_of(peers[i - 1])], slots.at[i - 1], send_s.at[i - 1], recv_s.at[i - 1],
                      peers[i - 1], c)

    def gather(i):
        return remote(wct.at[rows_of(r)], wct.at[rows_of(r)], send_g.at[i - 1], recv_g.at[i - 1],
                      peers[i - 1], c)

    for i in range(1, rows):
        scatter(i).start()
    total = part[rows_of(r), :]
    for i in range(1, rows):
        scatter(i).wait_recv()
        total = total + slots[i - 1]
    wct[rows_of(r), :] = total
    for i in range(1, rows):
        gather(i).start()

    def origin(h):
        return (r + rows * h) // 2

    def piece(h, i):
        return wrt.at[h, rows_of((r + rows - i) % rows)]

    def up(h, i):
        return remote(piece(h, i), piece(h, i), send_up.at[h, i], recv_z.at[h, i], r, c + 2)

    def down(h, i):
        return remote(piece(h, i), piece(h, i), send_down.at[h, i], recv_z.at[h, i], r, c - 2)

    def across(h, i):
        return remote(piece(h, i), piece(h, i), send_k.at[h, i], recv_z.at[h, i], r, c + 1 - 2 * k)

    for i in range(rows):
        if i:
            gather(i).wait_recv()
        for h in range(halves):
            @pl.when(c == r + rows * h)
            def _(h=h, i=i):
                place = rows_of((r + rows - i) % rows)
                wrt[h, place, :] = wct[place, :]
                pl.when(z < chips - 1)(lambda: up(h, i).start())
                pl.when(z > 0)(lambda: down(h, i).start())
                across(h, i).start()

    for i in range(rows):
        for h in range(halves):
            @pl.when(c != r + rows * h)
            def _(h=h, i=i):
                across(h, i).wait_recv()

                @pl.when(relay)
                def _():
                    pl.when((z > origin(h)) & (z < chips - 1))(lambda: up(h, i).start())
                    pl.when((z < origin(h)) & (z > 0))(lambda: down(h, i).start())
                    across(h, i).start()

    for i in range(1, rows):
        scatter(i).wait_send()
        gather(i).wait_send()

    @pl.when(relay)
    def _():
        for i in range(rows):
            for h in range(halves):
                pl.when((z >= origin(h)) & (z < chips - 1))(lambda: up(h, i).wait_send())
                pl.when((z <= origin(h)) & (z > 0))(lambda: down(h, i).wait_send())
                across(h, i).wait_send()


def reduce_product(panel, rows, cols, part):
    width, local_cols = part.shape
    halves = cols // rows
    dma = pltpu.SemaphoreType.DMA
    f32 = jnp.float32
    return pl.pallas_call(
        functools.partial(product_kernel, rows, cols),
        out_shape=(jax.ShapeDtypeStruct(part.shape, f32),
                   jax.ShapeDtypeStruct((halves, width, local_cols), f32)),
        in_specs=[VMEM],
        out_specs=(VMEM,) * 2,
        scratch_shapes=[pltpu.VMEM((rows - 1, width // rows, local_cols), f32),
                        dma((rows - 1,)), dma((rows - 1,)), dma((rows - 1,)), dma((rows - 1,)),
                        dma((halves, rows)), dma((halves, rows)), dma((halves, rows)), dma((halves, rows))],
        compiler_params=pltpu.CompilerParams(collective_id=PANELS + panel, has_side_effects=True,
                                             vmem_limit_bytes=40 * 2**20),
        name=f"reduce_product_{panel}",
    )(part)


def sum_kernel(rows, part, out, slots, send_s, recv_s, send_k, recv_k):
    r, c = lax.axis_index("row"), lax.axis_index("col")
    k = c % 2
    half = part.shape[0] // 2
    peers = [(r + i) % rows for i in range(1, rows)]
    greet([(True, peer, c) for peer in peers] + [(True, r, c + 1 - 2 * k)])
    mine = pl.ds(pl.multiple_of(k * half, half), half)

    def send(i):
        return remote(part.at[mine], slots.at[i - 1], send_s.at[i - 1], recv_s.at[i - 1], peers[i - 1], c)

    for i in range(1, rows):
        send(i).start()
    total = part[mine, :]
    for i in range(1, rows):
        send(i).wait()
        total = total + slots[i - 1]
    out[mine, :] = total
    swap = remote(out.at[mine], out.at[mine], send_k, recv_k, r, c + 1 - 2 * k)
    swap.start()
    swap.wait()


def sum_rows(panel, rows, part):
    dma = pltpu.SemaphoreType.DMA
    return pl.pallas_call(
        functools.partial(sum_kernel, rows),
        out_shape=jax.ShapeDtypeStruct(part.shape, jnp.float32),
        in_specs=[VMEM],
        out_specs=VMEM,
        scratch_shapes=[pltpu.VMEM((rows - 1, part.shape[0] // 2, part.shape[1]), jnp.float32),
                        dma((rows - 1,)), dma((rows - 1,)), dma, dma],
        compiler_params=pltpu.CompilerParams(collective_id=2 * PANELS + panel, has_side_effects=True,
                                             vmem_limit_bytes=32 * 2**20),
        name=f"sum_inner_{panel}",
    )(part)


def shards(matrix):
    row_blocks, width, col_blocks, _ = matrix.shape
    rows, cols = lax.axis_size("row"), lax.axis_size("col")
    halves = cols // rows
    row_index, col_index = lax.axis_index("row"), lax.axis_index("col")
    local_rows, local_cols = row_blocks * width, col_blocks * width
    dense = matrix.reshape(local_rows, local_cols)
    row_range = jnp.arange(local_rows, dtype=jnp.int32)
    col_range = jnp.arange(local_cols, dtype=jnp.int32)
    global_rows = (row_range // width * rows + row_index) * width + row_range % width
    global_cols = (col_range // width * cols + col_index) * width + col_range % width
    unit = jnp.arange(width, dtype=jnp.int32)
    for panel in range(PANELS):
        start = (panel + 1) * width
        col_slot, row_slot = panel // cols * width, panel // rows * width
        below = global_rows[:, None] >= start
        beside = global_cols[None, :] >= start
        low = jnp.where(below, dense[:, col_slot:col_slot + width], 0.0)
        right = jnp.where(beside, dense[row_slot:row_slot + width, :], 0.0)
        top_slot = (panel + 1) // rows * width
        xr, xct, gt = spread(panel, rows, cols, low, right, dot_tn(low, low),
                             low[top_slot:top_slot + width])
        upper, lower_inverse, coupling = factors(panel, gt)
        placed_rows = (global_rows[:, None] - start == unit[None, :]).astype(jnp.float32)
        placed_cols = (global_cols[None, :] - start == unit[:, None]).astype(jnp.float32)
        vec_rows = dot_nt(xr, lower_inverse) + placed_rows
        vec_cols = dot(lower_inverse, xct) + placed_cols
        part = lax.dot_general(vec_rows, dense, (((0,), (0,)), ((), ())), precision=high,
                               preferred_element_type=jnp.float32)
        part = jnp.where(beside, part, 0.0)
        applied_cols, applied = reduce_product(panel, rows, cols, part)
        applied = applied.reshape(halves, width, col_blocks, width)
        applied_rows = applied.transpose(2, 0, 3, 1).reshape(local_rows, width)
        inner = sum_rows(panel, rows, dot_tn(vec_rows, applied_rows))
        middle = dot_nt(dot(coupling, inner), coupling)
        factor_rows = dot_nt(applied_rows, coupling) - 0.5 * dot(vec_rows, middle)
        factor_cols = dot(coupling, applied_cols) - 0.5 * dot_tn(middle, vec_cols)
        dense = dense - dot(jnp.concatenate([factor_rows, vec_rows], axis=1),
                            jnp.concatenate([vec_cols, factor_cols], axis=0), high)
        old_col = dense[:, col_slot:col_slot + width]
        tiled = jnp.tile(-upper, (row_blocks, 1))
        on_top = (global_rows >= start) & (global_rows < start + width)
        new_col = jnp.where(below, jnp.where(on_top[:, None], tiled, 0.0), old_col)
        dense = dense.at[:, col_slot:col_slot + width].set(
            jnp.where(col_index == panel % cols, new_col, old_col))
        old_row = dense[row_slot:row_slot + width, :]
        tiled = jnp.tile(-upper.T, (1, col_blocks))
        on_top = (global_cols >= start) & (global_cols < start + width)
        new_row = jnp.where(beside, jnp.where(on_top[None, :], tiled, 0.0), old_row)
        dense = dense.at[row_slot:row_slot + width, :].set(
            jnp.where(row_index == panel % rows, new_row, old_row))
    return dense.reshape(matrix.shape)


def solution(mesh):
    assert mesh.shape["col"] % mesh.shape["row"] == 0 and mesh.shape["row"] % 2 == 0
    spec = P(None, "row", None, "col")
    return jax.shard_map(shards, mesh=mesh, in_specs=(spec,), out_specs=spec, check_vma=False)
```

```python
import functools

import jax
import jax.numpy as jnp
from jax import lax
from jax.experimental import pallas as pl
from jax.experimental.pallas import tpu as pltpu
from jax.sharding import PartitionSpec as P

PANELS = 2
MESH = pl.DeviceIdType.MESH
VMEM = pl.BlockSpec(memory_space=pltpu.VMEM)
highest = lax.Precision.HIGHEST
high = lax.Precision.HIGH


def dot(left, right, precision=highest):
    return jnp.dot(left, right, precision=precision, preferred_element_type=jnp.float32)


def dot_tn(left, right):
    return lax.dot_general(left, right, (((0,), (0,)), ((), ())), precision=highest,
                           preferred_element_type=jnp.float32)


def dot_nt(left, right):
    return lax.dot_general(left, right, (((1,), (1,)), ((), ())), precision=highest,
                           preferred_element_type=jnp.float32)


def remote(src, dst, send, recv, row, col):
    return pltpu.make_async_remote_copy(src_ref=src, dst_ref=dst, send_sem=send, recv_sem=recv,
                                        device_id=(row, col), device_id_type=MESH)


def greet(devices):
    barrier = pltpu.get_barrier_semaphore()
    for cond, row, col in devices:
        def hail(row=row, col=col):
            pl.semaphore_signal(barrier, inc=1, device_id=(row, col), device_id_type=MESH)
        if cond is True:
            hail()
        else:
            pl.when(cond)(hail)
    heard = sum(1 if cond is True else cond.astype(jnp.int32) for cond, _, _ in devices)
    pl.semaphore_wait(barrier, heard)


def ring_place(row, rows):
    return row + (row // 2) * (5 - 2 * row) if rows == 4 else row


RING_CHUNKS = 4


def spread_kernel(panel, rows, cols, xr_in, xct_in, gram_in, top_in, xr, xct, gt, slots,
                  send_z, send_k, recv_z, send_a, recv_a, send_b, recv_b,
                  send_g, recv_g, send_t, recv_t):
    width = gram_in.shape[0]
    r, c = lax.axis_index("row"), lax.axis_index("col")
    z, k, chips = c // 2, c % 2, cols // 2
    root_row, root_col, top_row = panel % rows, panel % cols, (panel + 1) % rows
    core = root_col % 2
    assert root_col // 2 == 0
    blocks = xr.shape[0] // width
    place = ring_place(r, rows)
    after = ring_place((place + 1) % rows, rows)
    before = ring_place((place + rows - 1) % rows, rows)
    ahead = (place - ring_place(root_row, rows) + rows) % rows
    behind = (rows - ahead) % rows
    peers = [(r + i) % rows for i in range(1, rows)]
    greet([(True, peer, c) for peer in peers]
          + [(True, r, c + 1 - 2 * k), (z > 0, r, c - 2), (z < chips - 1, r, c + 2)])

    owner = c == root_col
    relay = k == core

    def z_piece(i):
        if isinstance(i, int) and i >= blocks:
            return gt.at[i - blocks]
        return xr.at[pl.ds(i * width if isinstance(i, int) else pl.multiple_of(i * width, width), width)]

    def to_chip(i):
        return remote(z_piece(i), z_piece(i), send_z.at[i], recv_z.at[i], r, c + 2)

    def to_core(i):
        return remote(z_piece(i), z_piece(i), send_k.at[i], recv_z.at[i], r, c + 1 - 2 * k)

    def forward(i):
        pl.when(z < chips - 1)(lambda: to_chip(i).start())
        to_core(i).start()

    def gram_to(i, peer):
        return remote(gram_in, slots.at[i - 1], send_g.at[i - 1], recv_g.at[i - 1], peer, c)

    def top_to(i, peer):
        return remote(gt.at[1], gt.at[1], send_t.at[i - 1], recv_t, peer, c)

    half = width // 2
    step = half // RING_CHUNKS

    def ring_piece(side, i):
        return xct.at[pl.ds(side * half + i * step if isinstance(i, int) else pl.multiple_of(side * half + i * step, step), step)]

    def to_after(i):
        return remote(ring_piece(0, i), ring_piece(0, i), send_a.at[i], recv_a.at[i], after, c)

    def to_before(i):
        return remote(ring_piece(1, i), ring_piece(1, i), send_b.at[i], recv_b.at[i], before, c)

    @pl.when(owner)
    def _():
        for i, peer in enumerate(peers, 1):
            gram_to(i, peer).start()

        @pl.when(r == top_row)
        def _():
            gt[1] = top_in[...]
            for i, peer in enumerate(peers, 1):
                top_to(i, peer).start()

    @pl.when(ahead == 0)
    def _():
        xct[...] = xct_in[...]
        for i in range(RING_CHUNKS):
            to_after(i).start()
            to_before(i).start()

    @pl.when(owner)
    def _():
        for i in range(blocks):
            xr[pl.ds(i * width, width), :] = xr_in[pl.ds(i * width, width), :]
            forward(i)
        total = gram_in[...]
        for i, peer in enumerate(peers, 1):
            gram_to(i, peer).wait()
            total = total + slots[i - 1]
        gt[0] = total
        forward(blocks)

        @pl.when(r != top_row)
        def _():
            top_to(1, peers[0]).wait_recv()

        forward(blocks + 1)

    for t in range(max(blocks + 2 + chips - 1, RING_CHUNKS + rows - 2)):
        i_after, i_before, i_z = t + 1 - ahead, t + 1 - behind, t - z

        @pl.when((ahead != 0) & (i_after >= 0) & (i_after < RING_CHUNKS))
        def _(i=i_after):
            to_after(i).wait_recv()
            pl.when(ahead < rows - 1)(lambda: to_after(i).start())

        @pl.when((ahead != 0) & (i_before >= 0) & (i_before < RING_CHUNKS))
        def _(i=i_before):
            to_before(i).wait_recv()
            pl.when(behind < rows - 1)(lambda: to_before(i).start())

        @pl.when(jnp.logical_not(owner) & (i_z >= 0) & (i_z < blocks))
        def _(i=i_z):
            to_core(i).wait_recv()
            pl.when(relay)(lambda: forward(i))

        for extra in (blocks, blocks + 1):
            @pl.when(jnp.logical_not(owner) & (i_z == extra))
            def _(i=extra):
                to_core(i).wait_recv()
                pl.when(relay)(lambda: forward(i))

    @pl.when(owner & (r == top_row))
    def _():
        for i, peer in enumerate(peers, 1):
            top_to(i, peer).wait_send()

    @pl.when(relay)
    def _():
        for i in range(blocks + 2):
            pl.when(z < chips - 1)(lambda: to_chip(i).wait_send())
            to_core(i).wait_send()

    for i in range(RING_CHUNKS):
        pl.when(ahead < rows - 1)(lambda: to_after(i).wait_send())
        pl.when(behind < rows - 1)(lambda: to_before(i).wait_send())


def spread(panel, rows, cols, xr, xct, gram, top):
    width = gram.shape[0]
    pieces = xr.shape[0] // width + 2
    dma = pltpu.SemaphoreType.DMA
    f32 = jnp.float32
    return pl.pallas_call(
        functools.partial(spread_kernel, panel, rows, cols),
        out_shape=(jax.ShapeDtypeStruct(xr.shape, f32), jax.ShapeDtypeStruct(xct.shape, f32),
                   jax.ShapeDtypeStruct((2, width, width), f32)),
        in_specs=[VMEM] * 4,
        out_specs=(VMEM,) * 3,
        scratch_shapes=[pltpu.VMEM((rows - 1, width, width), f32),
                        dma((pieces,)), dma((pieces,)), dma((pieces,)),
                        dma((RING_CHUNKS,)), dma((RING_CHUNKS,)), dma((RING_CHUNKS,)), dma((RING_CHUNKS,)),
                        dma((rows - 1,)), dma((rows - 1,)), dma((rows - 1,)), dma],
        compiler_params=pltpu.CompilerParams(collective_id=panel, has_side_effects=True,
                                             vmem_limit_bytes=40 * 2**20),
        name=f"spread_panel_{panel}",
    )(xr, xct, gram, top)


GROUP = 4


def eliminate(block):
    size = block.shape[0]
    row = lax.broadcasted_iota(jnp.int32, (size, size), 0)
    col = lax.broadcasted_iota(jnp.int32, (size, size), 1)
    eye = (row == col).astype(jnp.float32)
    work = jnp.concatenate([block, eye], axis=1)
    lane_rows = lax.broadcasted_iota(jnp.int32, work.shape, 0)
    for base in range(0, size, GROUP):
        columns = [jnp.broadcast_to(work[:, base + i:base + i + 1], work.shape) for i in range(GROUP)]
        pivots = [work[base + i:base + i + 1, :] for i in range(GROUP)]
        change = None
        for i in range(GROUP):
            at = base + i
            inverse = 1.0 / columns[i][at:at + 1, :]
            factor = jnp.where(lane_rows > at, columns[i] * inverse, 0.0)
            for l in range(i + 1, GROUP):
                columns[l] = columns[l] - factor * columns[l][at:at + 1, :]
                pivots[l] = pivots[l] - factor[base + l:base + l + 1, :] * pivots[i]
            term = factor * pivots[i]
            change = term if change is None else change + term
        work = work - change
    diagonal = jnp.sum(jnp.where(row == col, work[:, :size], 0.0), axis=1, keepdims=True)
    return jnp.where(row >= col, work[:, size:] * lax.rsqrt(diagonal), 0.0)


def factorize(work, size):
    width = work.shape[0]
    for start in range(0, width, size):
        stop = start + size
        inverse = eliminate(work[start:stop, start:stop])
        strip = dot(inverse, work[start:stop, :])
        work[start:stop, :] = strip
        if stop < width:
            work[stop:, :] = work[stop:, :] - dot_tn(strip[:, stop:width], strip)


def factor_kernel(gt, upper, lower_inverse, coupling, work):
    width = upper.shape[0]
    row = lax.broadcasted_iota(jnp.int32, (width, width), 0)
    col = lax.broadcasted_iota(jnp.int32, (width, width), 1)
    eye = (row == col).astype(jnp.float32)
    work[:, :width] = gt[0]
    work[:, width:] = eye
    factorize(work, 64)
    upper[...] = jnp.where(row <= col, work[:, :width], 0.0)
    inverse = work[:, width:]
    lower_inverse[...] = inverse
    shifted = eye + dot_nt(gt[1], inverse)
    work[:, :width] = dot_tn(shifted, shifted)
    work[:, width:] = eye
    factorize(work, 64)
    inverse = work[:, width:]
    coupling[...] = dot_tn(inverse, dot_nt(inverse, shifted))


def factors(panel, gt):
    width = gt.shape[1]
    square = jax.ShapeDtypeStruct((width, width), jnp.float32)
    return pl.pallas_call(
        factor_kernel,
        out_shape=(square,) * 3,
        in_specs=[VMEM],
        out_specs=(VMEM,) * 3,
        scratch_shapes=[pltpu.VMEM((width, 2 * width), jnp.float32)],
        compiler_params=pltpu.CompilerParams(vmem_limit_bytes=32 * 2**20),
        name=f"factors_{panel}",
    )(gt)


def product_kernel(rows, cols, part, wct, wrt, slots, send_s, recv_s, send_g, recv_g,
                   send_up, send_down, send_k, recv_z):
    r, c = lax.axis_index("row"), lax.axis_index("col")
    z, k, chips = c // 2, c % 2, cols // 2
    share = part.shape[0] // rows
    halves = cols // rows
    relay = k == r % 2
    peers = [(r + i) % rows for i in range(1, rows)]
    greet([(True, peer, c) for peer in peers]
          + [(True, r, c + 1 - 2 * k), (z > 0, r, c - 2), (z < chips - 1, r, c + 2)])

    def rows_of(q):
        return pl.ds(pl.multiple_of(q * share, share), share)

    def scatter(i):
        return remote(part.at[rows_of(peers[i - 1])], slots.at[i - 1], send_s.at[i - 1], recv_s.at[i - 1],
                      peers[i - 1], c)

    def gather(i):
        return remote(wct.at[rows_of(r)], wct.at[rows_of(r)], send_g.at[i - 1], recv_g.at[i - 1],
                      peers[i - 1], c)

    for i in range(1, rows):
        scatter(i).start()
    total = part[rows_of(r), :]
    for i in range(1, rows):
        scatter(i).wait_recv()
        total = total + slots[i - 1]
    wct[rows_of(r), :] = total
    for i in range(1, rows):
        gather(i).start()

    def origin(h):
        return (r + rows * h) // 2

    def piece(h, i):
        return wrt.at[h, rows_of((r + rows - i) % rows)]

    def up(h, i):
        return remote(piece(h, i), piece(h, i), send_up.at[h, i], recv_z.at[h, i], r, c + 2)

    def down(h, i):
        return remote(piece(h, i), piece(h, i), send_down.at[h, i], recv_z.at[h, i], r, c - 2)

    def across(h, i):
        return remote(piece(h, i), piece(h, i), send_k.at[h, i], recv_z.at[h, i], r, c + 1 - 2 * k)

    for i in range(rows):
        if i:
            gather(i).wait_recv()
        for h in range(halves):
            @pl.when(c == r + rows * h)
            def _(h=h, i=i):
                place = rows_of((r + rows - i) % rows)
                wrt[h, place, :] = wct[place, :]
                pl.when(z < chips - 1)(lambda: up(h, i).start())
                pl.when(z > 0)(lambda: down(h, i).start())
                across(h, i).start()

    for i in range(rows):
        for h in range(halves):
            @pl.when(c != r + rows * h)
            def _(h=h, i=i):
                across(h, i).wait_recv()

                @pl.when(relay)
                def _():
                    pl.when((z > origin(h)) & (z < chips - 1))(lambda: up(h, i).start())
                    pl.when((z < origin(h)) & (z > 0))(lambda: down(h, i).start())
                    across(h, i).start()

    for i in range(1, rows):
        scatter(i).wait_send()
        gather(i).wait_send()

    @pl.when(relay)
    def _():
        for i in range(rows):
            for h in range(halves):
                pl.when((z >= origin(h)) & (z < chips - 1))(lambda: up(h, i).wait_send())
                pl.when((z <= origin(h)) & (z > 0))(lambda: down(h, i).wait_send())
                across(h, i).wait_send()


def reduce_product(panel, rows, cols, part):
    width, local_cols = part.shape
    halves = cols // rows
    dma = pltpu.SemaphoreType.DMA
    f32 = jnp.float32
    return pl.pallas_call(
        functools.partial(product_kernel, rows, cols),
        out_shape=(jax.ShapeDtypeStruct(part.shape, f32),
                   jax.ShapeDtypeStruct((halves, width, local_cols), f32)),
        in_specs=[VMEM],
        out_specs=(VMEM,) * 2,
        scratch_shapes=[pltpu.VMEM((rows - 1, width // rows, local_cols), f32),
                        dma((rows - 1,)), dma((rows - 1,)), dma((rows - 1,)), dma((rows - 1,)),
                        dma((halves, rows)), dma((halves, rows)), dma((halves, rows)), dma((halves, rows))],
        compiler_params=pltpu.CompilerParams(collective_id=PANELS + panel, has_side_effects=True,
                                             vmem_limit_bytes=40 * 2**20),
        name=f"reduce_product_{panel}",
    )(part)


def sum_kernel(rows, part, out, slots, send_s, recv_s, send_k, recv_k):
    r, c = lax.axis_index("row"), lax.axis_index("col")
    k = c % 2
    half = part.shape[0] // 2
    peers = [(r + i) % rows for i in range(1, rows)]
    greet([(True, peer, c) for peer in peers] + [(True, r, c + 1 - 2 * k)])
    mine = pl.ds(pl.multiple_of(k * half, half), half)

    def send(i):
        return remote(part.at[mine], slots.at[i - 1], send_s.at[i - 1], recv_s.at[i - 1], peers[i - 1], c)

    for i in range(1, rows):
        send(i).start()
    total = part[mine, :]
    for i in range(1, rows):
        send(i).wait()
        total = total + slots[i - 1]
    out[mine, :] = total
    swap = remote(out.at[mine], out.at[mine], send_k, recv_k, r, c + 1 - 2 * k)
    swap.start()
    swap.wait()


def sum_rows(panel, rows, part):
    dma = pltpu.SemaphoreType.DMA
    return pl.pallas_call(
        functools.partial(sum_kernel, rows),
        out_shape=jax.ShapeDtypeStruct(part.shape, jnp.float32),
        in_specs=[VMEM],
        out_specs=VMEM,
        scratch_shapes=[pltpu.VMEM((rows - 1, part.shape[0] // 2, part.shape[1]), jnp.float32),
                        dma((rows - 1,)), dma((rows - 1,)), dma, dma],
        compiler_params=pltpu.CompilerParams(collective_id=2 * PANELS + panel, has_side_effects=True,
                                             vmem_limit_bytes=32 * 2**20),
        name=f"sum_inner_{panel}",
    )(part)


def shards(matrix):
    row_blocks, width, col_blocks, _ = matrix.shape
    rows, cols = lax.axis_size("row"), lax.axis_size("col")
    halves = cols // rows
    row_index, col_index = lax.axis_index("row"), lax.axis_index("col")
    local_rows, local_cols = row_blocks * width, col_blocks * width
    dense = matrix.reshape(local_rows, local_cols)
    row_range = jnp.arange(local_rows, dtype=jnp.int32)
    col_range = jnp.arange(local_cols, dtype=jnp.int32)
    global_rows = (row_range // width * rows + row_index) * width + row_range % width
    global_cols = (col_range // width * cols + col_index) * width + col_range % width
    unit = jnp.arange(width, dtype=jnp.int32)
    for panel in range(PANELS):
        start = (panel + 1) * width
        col_slot, row_slot = panel // cols * width, panel // rows * width
        below = global_rows[:, None] >= start
        beside = global_cols[None, :] >= start
        low = jnp.where(below, dense[:, col_slot:col_slot + width], 0.0)
        right = jnp.where(beside, dense[row_slot:row_slot + width, :], 0.0)
        top_slot = (panel + 1) // rows * width
        xr, xct, gt = spread(panel, rows, cols, low, right, dot_tn(low, low),
                             low[top_slot:top_slot + width])
        upper, lower_inverse, coupling = factors(panel, gt)
        placed_rows = (global_rows[:, None] - start == unit[None, :]).astype(jnp.float32)
        placed_cols = (global_cols[None, :] - start == unit[:, None]).astype(jnp.float32)
        vec_rows = dot_nt(xr, lower_inverse) + placed_rows
        vec_cols = dot(lower_inverse, xct) + placed_cols
        part = lax.dot_general(vec_rows, dense, (((0,), (0,)), ((), ())), precision=high,
                               preferred_element_type=jnp.float32)
        part = jnp.where(beside, part, 0.0)
        applied_cols, applied = reduce_product(panel, rows, cols, part)
        applied = applied.reshape(halves, width, col_blocks, width)
        applied_rows = applied.transpose(2, 0, 3, 1).reshape(local_rows, width)
        inner = sum_rows(panel, rows, dot_tn(vec_rows, applied_rows))
        middle = dot_nt(dot(coupling, inner), coupling)
        factor_rows = dot_nt(applied_rows, coupling) - 0.5 * dot(vec_rows, middle)
        factor_cols = dot(coupling, applied_cols) - 0.5 * dot_tn(middle, vec_cols)
        dense = dense - dot(jnp.concatenate([factor_rows, vec_rows], axis=1),
                            jnp.concatenate([vec_cols, factor_cols], axis=0), high)
        old_col = dense[:, col_slot:col_slot + width]
        tiled = jnp.tile(-upper, (row_blocks, 1))
        on_top = (global_rows >= start) & (global_rows < start + width)
        new_col = jnp.where(below, jnp.where(on_top[:, None], tiled, 0.0), old_col)
        dense = dense.at[:, col_slot:col_slot + width].set(
            jnp.where(col_index == panel % cols, new_col, old_col))
        old_row = dense[row_slot:row_slot + width, :]
        tiled = jnp.tile(-upper.T, (1, col_blocks))
        on_top = (global_cols >= start) & (global_cols < start + width)
        new_row = jnp.where(beside, jnp.where(on_top[None, :], tiled, 0.0), old_row)
        dense = dense.at[row_slot:row_slot + width, :].set(
            jnp.where(row_index == panel % rows, new_row, old_row))
    return dense.reshape(matrix.shape)


def solution(mesh):
    assert mesh.shape["col"] % mesh.shape["row"] == 0 and mesh.shape["row"] % 2 == 0
    spec = P(None, "row", None, "col")
    return jax.shard_map(shards, mesh=mesh, in_specs=(spec,), out_specs=spec, check_vma=False)
```

```python
import functools

import jax
import jax.numpy as jnp
from jax import lax
from jax.experimental import pallas as pl
from jax.experimental.pallas import tpu as pltpu
from jax.sharding import PartitionSpec as P

PANELS = 2
MESH = pl.DeviceIdType.MESH
VMEM = pl.BlockSpec(memory_space=pltpu.VMEM)
highest = lax.Precision.HIGHEST
high = lax.Precision.HIGH


def dot(left, right, precision=highest):
    return jnp.dot(left, right, precision=precision, preferred_element_type=jnp.float32)


def dot_tn(left, right):
    return lax.dot_general(left, right, (((0,), (0,)), ((), ())), precision=highest,
                           preferred_element_type=jnp.float32)


def dot_nt(left, right):
    return lax.dot_general(left, right, (((1,), (1,)), ((), ())), precision=highest,
                           preferred_element_type=jnp.float32)


def remote(src, dst, send, recv, row, col):
    return pltpu.make_async_remote_copy(src_ref=src, dst_ref=dst, send_sem=send, recv_sem=recv,
                                        device_id=(row, col), device_id_type=MESH)


def greet(devices):
    barrier = pltpu.get_barrier_semaphore()
    for cond, row, col in devices:
        def hail(row=row, col=col):
            pl.semaphore_signal(barrier, inc=1, device_id=(row, col), device_id_type=MESH)
        if cond is True:
            hail()
        else:
            pl.when(cond)(hail)
    heard = sum(1 if cond is True else cond.astype(jnp.int32) for cond, _, _ in devices)
    pl.semaphore_wait(barrier, heard)


def ring_place(row, rows):
    return row + (row // 2) * (5 - 2 * row) if rows == 4 else row


GROUP = 4


def eliminate(block):
    size = block.shape[0]
    row = lax.broadcasted_iota(jnp.int32, (size, size), 0)
    col = lax.broadcasted_iota(jnp.int32, (size, size), 1)
    eye = (row == col).astype(jnp.float32)
    work = jnp.concatenate([block, eye], axis=1)
    lane_rows = lax.broadcasted_iota(jnp.int32, work.shape, 0)
    for base in range(0, size, GROUP):
        columns = [jnp.broadcast_to(work[:, base + i:base + i + 1], work.shape) for i in range(GROUP)]
        pivots = [work[base + i:base + i + 1, :] for i in range(GROUP)]
        change = None
        for i in range(GROUP):
            at = base + i
            inverse = 1.0 / columns[i][at:at + 1, :]
            factor = jnp.where(lane_rows > at, columns[i] * inverse, 0.0)
            for l in range(i + 1, GROUP):
                columns[l] = columns[l] - factor * columns[l][at:at + 1, :]
                pivots[l] = pivots[l] - factor[base + l:base + l + 1, :] * pivots[i]
            term = factor * pivots[i]
            change = term if change is None else change + term
        work = work - change
    diagonal = jnp.sum(jnp.where(row == col, work[:, :size], 0.0), axis=1, keepdims=True)
    return jnp.where(row >= col, work[:, size:] * lax.rsqrt(diagonal), 0.0)


def factor_steps(work, size):
    width = work.shape[0]

    def step(start):
        stop = start + size
        inverse = eliminate(work[start:stop, start:stop])
        strip = dot(inverse, work[start:stop, :])
        work[start:stop, :] = strip
        if stop < width:
            work[stop:, :] = work[stop:, :] - dot_tn(strip[:, stop:width], strip)

    return [functools.partial(step, start) for start in range(0, width, size)]


def identity(width):
    row = lax.broadcasted_iota(jnp.int32, (width, width), 0)
    col = lax.broadcasted_iota(jnp.int32, (width, width), 1)
    return (row == col).astype(jnp.float32), row <= col


def cholesky_steps(gram, upper, lower_inverse, work):
    width = upper.shape[0]

    def begin():
        work[:, :width] = gram[...]
        work[:, width:] = identity(width)[0]

    def end():
        upper[...] = jnp.where(identity(width)[1], work[:, :width], 0.0)
        lower_inverse[...] = work[:, width:]

    return [begin] + factor_steps(work, 64) + [end]


def coupling_steps(top, lower_inverse, coupling, shifted, work):
    width = coupling.shape[0]

    def begin():
        eye = identity(width)[0]
        shifted[...] = eye + dot_nt(top[...], lower_inverse[...])
        work[:, :width] = dot_tn(shifted[...], shifted[...])
        work[:, width:] = eye

    def end():
        inverse = work[:, width:]
        coupling[...] = dot_tn(inverse, dot_nt(inverse, shifted[...]))

    return [begin] + factor_steps(work, 64) + [end]


RING_CHUNKS = 4
LEAD = 2


def spread_kernel(panel, rows, cols, xr_in, xct_in, gram_in, top_in, xr, xct, gt, upper, lower_inverse,
                  slots, work,
                  send_z, send_k, recv_z, send_a, recv_a, send_b, recv_b,
                  send_g, recv_g, send_t, recv_t):
    width = gram_in.shape[0]
    r, c = lax.axis_index("row"), lax.axis_index("col")
    z, k, chips = c // 2, c % 2, cols // 2
    root_row, root_col, top_row = panel % rows, panel % cols, (panel + 1) % rows
    core = root_col % 2
    assert root_col // 2 == 0
    blocks = xr.shape[0] // width
    place = ring_place(r, rows)
    after = ring_place((place + 1) % rows, rows)
    before = ring_place((place + rows - 1) % rows, rows)
    ahead = (place - ring_place(root_row, rows) + rows) % rows
    behind = (rows - ahead) % rows
    peers = [(r + i) % rows for i in range(1, rows)]
    greet([(True, peer, c) for peer in peers]
          + [(True, r, c + 1 - 2 * k), (z > 0, r, c - 2), (z < chips - 1, r, c + 2)])

    owner = c == root_col
    relay = k == core

    def z_piece(i):
        if isinstance(i, int):
            if i in (LEAD, LEAD + 1):
                return gt.at[i - LEAD]
            return xr.at[pl.ds((i if i < LEAD else i - 2) * width, width)]
        place = i - 2 * (i > LEAD).astype(jnp.int32)
        return xr.at[pl.ds(pl.multiple_of(place * width, width), width)]

    def to_chip(i):
        return remote(z_piece(i), z_piece(i), send_z.at[i], recv_z.at[i], r, c + 2)

    def to_core(i):
        return remote(z_piece(i), z_piece(i), send_k.at[i], recv_z.at[i], r, c + 1 - 2 * k)

    def forward(i):
        pl.when(z < chips - 1)(lambda: to_chip(i).start())
        to_core(i).start()

    def gram_to(i, peer):
        return remote(gram_in, slots.at[i - 1], send_g.at[i - 1], recv_g.at[i - 1], peer, c)

    def top_to(i, peer):
        return remote(gt.at[1], gt.at[1], send_t.at[i - 1], recv_t, peer, c)

    half = width // 2
    step = half // RING_CHUNKS

    def ring_piece(side, i):
        return xct.at[pl.ds(side * half + i * step if isinstance(i, int) else pl.multiple_of(side * half + i * step, step), step)]

    def to_after(i):
        return remote(ring_piece(0, i), ring_piece(0, i), send_a.at[i], recv_a.at[i], after, c)

    def to_before(i):
        return remote(ring_piece(1, i), ring_piece(1, i), send_b.at[i], recv_b.at[i], before, c)

    @pl.when(owner)
    def _():
        for i, peer in enumerate(peers, 1):
            gram_to(i, peer).start()

        @pl.when(r == top_row)
        def _():
            gt[1] = top_in[...]
            for i, peer in enumerate(peers, 1):
                top_to(i, peer).start()

    @pl.when(ahead == 0)
    def _():
        xct[...] = xct_in[...]
        for i in range(RING_CHUNKS):
            to_after(i).start()
            to_before(i).start()

    @pl.when(owner)
    def _():
        for i in range(LEAD):
            xr[pl.ds(i * width, width), :] = xr_in[pl.ds(i * width, width), :]
            forward(i)
        total = gram_in[...]
        for i, peer in enumerate(peers, 1):
            gram_to(i, peer).wait()
            total = total + slots[i - 1]
        gt[0] = total
        forward(LEAD)

        @pl.when(r != top_row)
        def _():
            top_to(1, peers[0]).wait_recv()

        forward(LEAD + 1)
        for i in range(LEAD, blocks):
            xr[pl.ds(i * width, width), :] = xr_in[pl.ds(i * width, width), :]
            forward(i + 2)

    steps = cholesky_steps(gt.at[0], upper, lower_inverse, work)
    for t in range(max(blocks + 2 + chips - 1, RING_CHUNKS + rows - 2)):
        i_after, i_before, i_z = t + 1 - ahead, t + 1 - behind, t - z

        @pl.when((ahead != 0) & (i_after >= 0) & (i_after < RING_CHUNKS))
        def _(i=i_after):
            to_after(i).wait_recv()
            pl.when(ahead < rows - 1)(lambda: to_after(i).start())

        @pl.when((ahead != 0) & (i_before >= 0) & (i_before < RING_CHUNKS))
        def _(i=i_before):
            to_before(i).wait_recv()
            pl.when(behind < rows - 1)(lambda: to_before(i).start())

        body = (i_z >= 0) & (i_z < blocks + 2) & ((i_z < LEAD) | (i_z > LEAD + 1))

        @pl.when(jnp.logical_not(owner) & body)
        def _(i=i_z):
            to_core(i).wait_recv()
            pl.when(relay)(lambda: forward(i))

        for extra in (LEAD, LEAD + 1):
            @pl.when(jnp.logical_not(owner) & (i_z == extra))
            def _(i=extra):
                to_core(i).wait_recv()
                pl.when(relay)(lambda: forward(i))

        if steps and t >= LEAD + chips:
            steps.pop(0)()

    for step_left in steps:
        step_left()

    @pl.when(owner & (r == top_row))
    def _():
        for i, peer in enumerate(peers, 1):
            top_to(i, peer).wait_send()

    @pl.when(relay)
    def _():
        for i in range(blocks + 2):
            pl.when(z < chips - 1)(lambda: to_chip(i).wait_send())
            to_core(i).wait_send()

    for i in range(RING_CHUNKS):
        pl.when(ahead < rows - 1)(lambda: to_after(i).wait_send())
        pl.when(behind < rows - 1)(lambda: to_before(i).wait_send())


def spread(panel, rows, cols, xr, xct, gram, top):
    width = gram.shape[0]
    pieces = xr.shape[0] // width + 2
    dma = pltpu.SemaphoreType.DMA
    f32 = jnp.float32
    return pl.pallas_call(
        functools.partial(spread_kernel, panel, rows, cols),
        out_shape=(jax.ShapeDtypeStruct(xr.shape, f32), jax.ShapeDtypeStruct(xct.shape, f32),
                   jax.ShapeDtypeStruct((2, width, width), f32),
                   jax.ShapeDtypeStruct((width, width), f32), jax.ShapeDtypeStruct((width, width), f32)),
        in_specs=[VMEM] * 4,
        out_specs=(VMEM,) * 5,
        scratch_shapes=[pltpu.VMEM((rows - 1, width, width), f32), pltpu.VMEM((width, 2 * width), f32),
                        dma((pieces,)), dma((pieces,)), dma((pieces,)),
                        dma((RING_CHUNKS,)), dma((RING_CHUNKS,)), dma((RING_CHUNKS,)), dma((RING_CHUNKS,)),
                        dma((rows - 1,)), dma((rows - 1,)), dma((rows - 1,)), dma],
        compiler_params=pltpu.CompilerParams(collective_id=panel, has_side_effects=True,
                                             vmem_limit_bytes=40 * 2**20),
        name=f"spread_panel_{panel}",
    )(xr, xct, gram, top)


def product_kernel(rows, cols, part, top, lower_inverse, wct, wrt, coupling, slots, work, shifted, send_s, recv_s, send_g, recv_g,
                   send_up, send_down, send_k, recv_z):
    r, c = lax.axis_index("row"), lax.axis_index("col")
    z, k, chips = c // 2, c % 2, cols // 2
    share = part.shape[0] // rows
    halves = cols // rows
    relay = k == r % 2
    peers = [(r + i) % rows for i in range(1, rows)]
    greet([(True, peer, c) for peer in peers]
          + [(True, r, c + 1 - 2 * k), (z > 0, r, c - 2), (z < chips - 1, r, c + 2)])

    def rows_of(q):
        return pl.ds(pl.multiple_of(q * share, share), share)

    def scatter(i):
        return remote(part.at[rows_of(peers[i - 1])], slots.at[i - 1], send_s.at[i - 1], recv_s.at[i - 1],
                      peers[i - 1], c)

    def gather(i):
        return remote(wct.at[rows_of(r)], wct.at[rows_of(r)], send_g.at[i - 1], recv_g.at[i - 1],
                      peers[i - 1], c)

    for i in range(1, rows):
        scatter(i).start()
    steps = coupling_steps(top, lower_inverse, coupling, shifted, work)
    steps.pop(0)()
    steps.pop(0)()
    total = part[rows_of(r), :]
    for i in range(1, rows):
        scatter(i).wait_recv()
        total = total + slots[i - 1]
    wct[rows_of(r), :] = total
    for i in range(1, rows):
        gather(i).start()
    steps.pop(0)()

    def origin(h):
        return (r + rows * h) // 2

    def piece(h, i):
        return wrt.at[h, rows_of((r + rows - i) % rows)]

    def up(h, i):
        return remote(piece(h, i), piece(h, i), send_up.at[h, i], recv_z.at[h, i], r, c + 2)

    def down(h, i):
        return remote(piece(h, i), piece(h, i), send_down.at[h, i], recv_z.at[h, i], r, c - 2)

    def across(h, i):
        return remote(piece(h, i), piece(h, i), send_k.at[h, i], recv_z.at[h, i], r, c + 1 - 2 * k)

    for i in range(rows):
        if i:
            gather(i).wait_recv()
        for h in range(halves):
            @pl.when(c == r + rows * h)
            def _(h=h, i=i):
                place = rows_of((r + rows - i) % rows)
                wrt[h, place, :] = wct[place, :]
                pl.when(z < chips - 1)(lambda: up(h, i).start())
                pl.when(z > 0)(lambda: down(h, i).start())
                across(h, i).start()

    for i in range(rows):
        for h in range(halves):
            @pl.when(c != r + rows * h)
            def _(h=h, i=i):
                across(h, i).wait_recv()

                @pl.when(relay)
                def _():
                    pl.when((z > origin(h)) & (z < chips - 1))(lambda: up(h, i).start())
                    pl.when((z < origin(h)) & (z > 0))(lambda: down(h, i).start())
                    across(h, i).start()
        if steps:
            steps.pop(0)()

    for step_left in steps:
        step_left()

    for i in range(1, rows):
        scatter(i).wait_send()
        gather(i).wait_send()

    @pl.when(relay)
    def _():
        for i in range(rows):
            for h in range(halves):
                pl.when((z >= origin(h)) & (z < chips - 1))(lambda: up(h, i).wait_send())
                pl.when((z <= origin(h)) & (z > 0))(lambda: down(h, i).wait_send())
                across(h, i).wait_send()


def reduce_product(panel, rows, cols, part, top, lower_inverse):
    width, local_cols = part.shape
    halves = cols // rows
    dma = pltpu.SemaphoreType.DMA
    f32 = jnp.float32
    return pl.pallas_call(
        functools.partial(product_kernel, rows, cols),
        out_shape=(jax.ShapeDtypeStruct(part.shape, f32),
                   jax.ShapeDtypeStruct((halves, width, local_cols), f32),
                   jax.ShapeDtypeStruct((width, width), f32)),
        in_specs=[VMEM] * 3,
        out_specs=(VMEM,) * 3,
        scratch_shapes=[pltpu.VMEM((rows - 1, width // rows, local_cols), f32),
                        pltpu.VMEM((width, 2 * width), f32), pltpu.VMEM((width, width), f32),
                        dma((rows - 1,)), dma((rows - 1,)), dma((rows - 1,)), dma((rows - 1,)),
                        dma((halves, rows)), dma((halves, rows)), dma((halves, rows)), dma((halves, rows))],
        compiler_params=pltpu.CompilerParams(collective_id=PANELS + panel, has_side_effects=True,
                                             vmem_limit_bytes=40 * 2**20),
        name=f"reduce_product_{panel}",
    )(part, top, lower_inverse)


def sum_kernel(rows, part, out, slots, send_s, recv_s, send_k, recv_k):
    r, c = lax.axis_index("row"), lax.axis_index("col")
    k = c % 2
    half = part.shape[0] // 2
    peers = [(r + i) % rows for i in range(1, rows)]
    greet([(True, peer, c) for peer in peers] + [(True, r, c + 1 - 2 * k)])
    mine = pl.ds(pl.multiple_of(k * half, half), half)

    def send(i):
        return remote(part.at[mine], slots.at[i - 1], send_s.at[i - 1], recv_s.at[i - 1], peers[i - 1], c)

    for i in range(1, rows):
        send(i).start()
    total = part[mine, :]
    for i in range(1, rows):
        send(i).wait()
        total = total + slots[i - 1]
    out[mine, :] = total
    swap = remote(out.at[mine], out.at[mine], send_k, recv_k, r, c + 1 - 2 * k)
    swap.start()
    swap.wait()


def sum_rows(panel, rows, part):
    dma = pltpu.SemaphoreType.DMA
    return pl.pallas_call(
        functools.partial(sum_kernel, rows),
        out_shape=jax.ShapeDtypeStruct(part.shape, jnp.float32),
        in_specs=[VMEM],
        out_specs=VMEM,
        scratch_shapes=[pltpu.VMEM((rows - 1, part.shape[0] // 2, part.shape[1]), jnp.float32),
                        dma((rows - 1,)), dma((rows - 1,)), dma, dma],
        compiler_params=pltpu.CompilerParams(collective_id=2 * PANELS + panel, has_side_effects=True,
                                             vmem_limit_bytes=32 * 2**20),
        name=f"sum_inner_{panel}",
    )(part)


def shards(matrix):
    row_blocks, width, col_blocks, _ = matrix.shape
    rows, cols = lax.axis_size("row"), lax.axis_size("col")
    halves = cols // rows
    row_index, col_index = lax.axis_index("row"), lax.axis_index("col")
    local_rows, local_cols = row_blocks * width, col_blocks * width
    dense = matrix.reshape(local_rows, local_cols)
    row_range = jnp.arange(local_rows, dtype=jnp.int32)
    col_range = jnp.arange(local_cols, dtype=jnp.int32)
    global_rows = (row_range // width * rows + row_index) * width + row_range % width
    global_cols = (col_range // width * cols + col_index) * width + col_range % width
    unit = jnp.arange(width, dtype=jnp.int32)
    for panel in range(PANELS):
        start = (panel + 1) * width
        col_slot, row_slot = panel // cols * width, panel // rows * width
        below = global_rows[:, None] >= start
        beside = global_cols[None, :] >= start
        low = jnp.where(below, dense[:, col_slot:col_slot + width], 0.0)
        right = jnp.where(beside, dense[row_slot:row_slot + width, :], 0.0)
        top_slot = (panel + 1) // rows * width
        xr, xct, gt, upper, lower_inverse = spread(panel, rows, cols, low, right, dot_tn(low, low),
                                                   low[top_slot:top_slot + width])
        placed_rows = (global_rows[:, None] - start == unit[None, :]).astype(jnp.float32)
        placed_cols = (global_cols[None, :] - start == unit[:, None]).astype(jnp.float32)
        vec_rows = dot_nt(xr, lower_inverse) + placed_rows
        vec_cols = dot(lower_inverse, xct) + placed_cols
        part = lax.dot_general(vec_rows, dense, (((0,), (0,)), ((), ())), precision=high,
                               preferred_element_type=jnp.float32)
        part = jnp.where(beside, part, 0.0)
        applied_cols, applied, coupling = reduce_product(panel, rows, cols, part, gt[1], lower_inverse)
        applied = applied.reshape(halves, width, col_blocks, width)
        applied_rows = applied.transpose(2, 0, 3, 1).reshape(local_rows, width)
        inner = sum_rows(panel, rows, dot_tn(vec_rows, applied_rows))
        middle = dot_nt(dot(coupling, inner), coupling)
        factor_rows = dot_nt(applied_rows, coupling) - 0.5 * dot(vec_rows, middle)
        factor_cols = dot(coupling, applied_cols) - 0.5 * dot_tn(middle, vec_cols)
        dense = dense - dot(jnp.concatenate([factor_rows, vec_rows], axis=1),
                            jnp.concatenate([vec_cols, factor_cols], axis=0), high)
        old_col = dense[:, col_slot:col_slot + width]
        tiled = jnp.tile(-upper, (row_blocks, 1))
        on_top = (global_rows >= start) & (global_rows < start + width)
        new_col = jnp.where(below, jnp.where(on_top[:, None], tiled, 0.0), old_col)
        dense = dense.at[:, col_slot:col_slot + width].set(
            jnp.where(col_index == panel % cols, new_col, old_col))
        old_row = dense[row_slot:row_slot + width, :]
        tiled = jnp.tile(-upper.T, (1, col_blocks))
        on_top = (global_cols >= start) & (global_cols < start + width)
        new_row = jnp.where(beside, jnp.where(on_top[None, :], tiled, 0.0), old_row)
        dense = dense.at[row_slot:row_slot + width, :].set(
            jnp.where(row_index == panel % rows, new_row, old_row))
    return dense.reshape(matrix.shape)


def solution(mesh):
    assert mesh.shape["col"] % mesh.shape["row"] == 0 and mesh.shape["row"] % 2 == 0
    spec = P(None, "row", None, "col")
    return jax.shard_map(shards, mesh=mesh, in_specs=(spec,), out_specs=spec, check_vma=False)
```

```python
import functools

import jax
import jax.numpy as jnp
from jax import lax
from jax.experimental import pallas as pl
from jax.experimental.pallas import tpu as pltpu
from jax.sharding import PartitionSpec as P

PANELS = 2
MESH = pl.DeviceIdType.MESH
VMEM = pl.BlockSpec(memory_space=pltpu.VMEM)
highest = lax.Precision.HIGHEST
high = lax.Precision.HIGH


def dot(left, right, precision=highest):
    return jnp.dot(left, right, precision=precision, preferred_element_type=jnp.float32)


def dot_tn(left, right):
    return lax.dot_general(left, right, (((0,), (0,)), ((), ())), precision=highest,
                           preferred_element_type=jnp.float32)


def dot_nt(left, right):
    return lax.dot_general(left, right, (((1,), (1,)), ((), ())), precision=highest,
                           preferred_element_type=jnp.float32)


def remote(src, dst, send, recv, row, col):
    return pltpu.make_async_remote_copy(src_ref=src, dst_ref=dst, send_sem=send, recv_sem=recv,
                                        device_id=(row, col), device_id_type=MESH)


def greet(devices):
    barrier = pltpu.get_barrier_semaphore()
    for cond, row, col in devices:
        def hail(row=row, col=col):
            pl.semaphore_signal(barrier, inc=1, device_id=(row, col), device_id_type=MESH)
        if cond is True:
            hail()
        else:
            pl.when(cond)(hail)
    heard = sum(1 if cond is True else cond.astype(jnp.int32) for cond, _, _ in devices)
    pl.semaphore_wait(barrier, heard)


def ring_place(row, rows):
    return row + (row // 2) * (5 - 2 * row) if rows == 4 else row


GROUP = 4


def eliminate(block):
    size = block.shape[0]
    row = lax.broadcasted_iota(jnp.int32, (size, size), 0)
    col = lax.broadcasted_iota(jnp.int32, (size, size), 1)
    eye = (row == col).astype(jnp.float32)
    work = jnp.concatenate([block, eye], axis=1)
    lane_rows = lax.broadcasted_iota(jnp.int32, work.shape, 0)
    for base in range(0, size, GROUP):
        columns = [jnp.broadcast_to(work[:, base + i:base + i + 1], work.shape) for i in range(GROUP)]
        pivots = [work[base + i:base + i + 1, :] for i in range(GROUP)]
        change = None
        for i in range(GROUP):
            at = base + i
            inverse = 1.0 / columns[i][at:at + 1, :]
            factor = jnp.where(lane_rows > at, columns[i] * inverse, 0.0)
            for l in range(i + 1, GROUP):
                columns[l] = columns[l] - factor * columns[l][at:at + 1, :]
                pivots[l] = pivots[l] - factor[base + l:base + l + 1, :] * pivots[i]
            term = factor * pivots[i]
            change = term if change is None else change + term
        work = work - change
    diagonal = jnp.sum(jnp.where(row == col, work[:, :size], 0.0), axis=1, keepdims=True)
    return jnp.where(row >= col, work[:, size:] * lax.rsqrt(diagonal), 0.0)


def factor_steps(work, size):
    width = work.shape[0]

    def step(start):
        stop = start + size
        inverse = eliminate(work[start:stop, start:stop])
        strip = dot(inverse, work[start:stop, :])
        work[start:stop, :] = strip
        if stop < width:
            work[stop:, :] = work[stop:, :] - dot_tn(strip[:, stop:width], strip)

    return [functools.partial(step, start) for start in range(0, width, size)]


def identity(width):
    row = lax.broadcasted_iota(jnp.int32, (width, width), 0)
    col = lax.broadcasted_iota(jnp.int32, (width, width), 1)
    return (row == col).astype(jnp.float32), row <= col


def cholesky_steps(gram, upper, lower_inverse, work):
    width = upper.shape[0]

    def begin():
        work[:, :width] = gram[...]
        work[:, width:] = identity(width)[0]

    def end():
        upper[...] = jnp.where(identity(width)[1], work[:, :width], 0.0)
        lower_inverse[...] = work[:, width:]

    return [begin] + factor_steps(work, 64) + [end]


def coupling_steps(top, lower_inverse, coupling, shifted, work):
    width = coupling.shape[0]

    def begin():
        eye = identity(width)[0]
        shifted[...] = eye + dot_nt(top[...], lower_inverse[...])
        work[:, :width] = dot_tn(shifted[...], shifted[...])
        work[:, width:] = eye

    def end():
        inverse = work[:, width:]
        coupling[...] = dot_tn(inverse, dot_nt(inverse, shifted[...]))

    return [begin] + factor_steps(work, 64) + [end]


RING_CHUNKS = 4
LEAD = 2


def spread_kernel(panel, rows, cols, xr_in, xct_in, gram_in, top_in, xr, xct, gt, upper, lower_inverse,
                  slots, work,
                  send_z, send_k, recv_z, send_a, recv_a, send_b, recv_b,
                  send_g, recv_g, send_t, recv_t):
    width = gram_in.shape[0]
    r, c = lax.axis_index("row"), lax.axis_index("col")
    z, k, chips = c // 2, c % 2, cols // 2
    root_row, root_col, top_row = panel % rows, panel % cols, (panel + 1) % rows
    core = root_col % 2
    assert root_col // 2 == 0
    blocks = xr.shape[0] // width
    place = ring_place(r, rows)
    after = ring_place((place + 1) % rows, rows)
    before = ring_place((place + rows - 1) % rows, rows)
    ahead = (place - ring_place(root_row, rows) + rows) % rows
    behind = (rows - ahead) % rows
    peers = [(r + i) % rows for i in range(1, rows)]
    greet([(True, peer, c) for peer in peers]
          + [(True, r, c + 1 - 2 * k), (z > 0, r, c - 2), (z < chips - 1, r, c + 2)])

    owner = c == root_col
    relay = k == core

    def z_piece(i):
        if isinstance(i, int):
            if i in (LEAD, LEAD + 1):
                return gt.at[i - LEAD]
            return xr.at[pl.ds((i if i < LEAD else i - 2) * width, width)]
        place = i - 2 * (i > LEAD).astype(jnp.int32)
        return xr.at[pl.ds(pl.multiple_of(place * width, width), width)]

    def to_chip(i):
        return remote(z_piece(i), z_piece(i), send_z.at[i], recv_z.at[i], r, c + 2)

    def to_core(i):
        return remote(z_piece(i), z_piece(i), send_k.at[i], recv_z.at[i], r, c + 1 - 2 * k)

    def forward(i):
        pl.when(z < chips - 1)(lambda: to_chip(i).start())
        to_core(i).start()

    def gram_to(i, peer):
        return remote(gram_in, slots.at[i - 1], send_g.at[i - 1], recv_g.at[i - 1], peer, c)

    def top_to(i, peer):
        return remote(gt.at[1], gt.at[1], send_t.at[i - 1], recv_t, peer, c)

    half = width // 2
    step = half // RING_CHUNKS

    def ring_piece(side, i):
        return xct.at[pl.ds(side * half + i * step if isinstance(i, int) else pl.multiple_of(side * half + i * step, step), step)]

    def to_after(i):
        return remote(ring_piece(0, i), ring_piece(0, i), send_a.at[i], recv_a.at[i], after, c)

    def to_before(i):
        return remote(ring_piece(1, i), ring_piece(1, i), send_b.at[i], recv_b.at[i], before, c)

    @pl.when(owner)
    def _():
        for i, peer in enumerate(peers, 1):
            gram_to(i, peer).start()

        @pl.when(r == top_row)
        def _():
            gt[1] = top_in[...]
            for i, peer in enumerate(peers, 1):
                top_to(i, peer).start()

    @pl.when(ahead == 0)
    def _():
        xct[...] = xct_in[...]
        for i in range(RING_CHUNKS):
            to_after(i).start()
            to_before(i).start()

    @pl.when(owner)
    def _():
        for i in range(LEAD):
            xr[pl.ds(i * width, width), :] = xr_in[pl.ds(i * width, width), :]
            forward(i)
        total = gram_in[...]
        for i, peer in enumerate(peers, 1):
            gram_to(i, peer).wait()
            total = total + slots[i - 1]
        gt[0] = total
        forward(LEAD)

        @pl.when(r != top_row)
        def _():
            top_to(1, peers[0]).wait_recv()

        forward(LEAD + 1)
        for i in range(LEAD, blocks):
            xr[pl.ds(i * width, width), :] = xr_in[pl.ds(i * width, width), :]
            forward(i + 2)

    steps = cholesky_steps(gt.at[0], upper, lower_inverse, work)
    for t in range(max(blocks + 2 + chips - 1, RING_CHUNKS + rows - 2)):
        i_after, i_before, i_z = t + 1 - ahead, t + 1 - behind, t - z

        @pl.when((ahead != 0) & (i_after >= 0) & (i_after < RING_CHUNKS))
        def _(i=i_after):
            to_after(i).wait_recv()
            pl.when(ahead < rows - 1)(lambda: to_after(i).start())

        @pl.when((ahead != 0) & (i_before >= 0) & (i_before < RING_CHUNKS))
        def _(i=i_before):
            to_before(i).wait_recv()
            pl.when(behind < rows - 1)(lambda: to_before(i).start())

        body = (i_z >= 0) & (i_z < blocks + 2) & ((i_z < LEAD) | (i_z > LEAD + 1))

        @pl.when(jnp.logical_not(owner) & body)
        def _(i=i_z):
            to_core(i).wait_recv()
            pl.when(relay)(lambda: forward(i))

        for extra in (LEAD, LEAD + 1):
            @pl.when(jnp.logical_not(owner) & (i_z == extra))
            def _(i=extra):
                to_core(i).wait_recv()
                pl.when(relay)(lambda: forward(i))

        if steps and t >= LEAD + chips:
            steps.pop(0)()

    for step_left in steps:
        step_left()

    @pl.when(owner & (r == top_row))
    def _():
        for i, peer in enumerate(peers, 1):
            top_to(i, peer).wait_send()

    @pl.when(relay)
    def _():
        for i in range(blocks + 2):
            pl.when(z < chips - 1)(lambda: to_chip(i).wait_send())
            to_core(i).wait_send()

    for i in range(RING_CHUNKS):
        pl.when(ahead < rows - 1)(lambda: to_after(i).wait_send())
        pl.when(behind < rows - 1)(lambda: to_before(i).wait_send())


def spread(panel, rows, cols, xr, xct, gram, top):
    width = gram.shape[0]
    pieces = xr.shape[0] // width + 2
    dma = pltpu.SemaphoreType.DMA
    f32 = jnp.float32
    return pl.pallas_call(
        functools.partial(spread_kernel, panel, rows, cols),
        out_shape=(jax.ShapeDtypeStruct(xr.shape, f32), jax.ShapeDtypeStruct(xct.shape, f32),
                   jax.ShapeDtypeStruct((2, width, width), f32),
                   jax.ShapeDtypeStruct((width, width), f32), jax.ShapeDtypeStruct((width, width), f32)),
        in_specs=[VMEM] * 4,
        out_specs=(VMEM,) * 5,
        scratch_shapes=[pltpu.VMEM((rows - 1, width, width), f32), pltpu.VMEM((width, 2 * width), f32),
                        dma((pieces,)), dma((pieces,)), dma((pieces,)),
                        dma((RING_CHUNKS,)), dma((RING_CHUNKS,)), dma((RING_CHUNKS,)), dma((RING_CHUNKS,)),
                        dma((rows - 1,)), dma((rows - 1,)), dma((rows - 1,)), dma],
        compiler_params=pltpu.CompilerParams(collective_id=panel, has_side_effects=True,
                                             vmem_limit_bytes=40 * 2**20),
        name=f"spread_panel_{panel}",
    )(xr, xct, gram, top)


def product_kernel(rows, cols, part, top, lower_inverse, vec_cols, wct, wrt, coupling, inner, slots, work, shifted,
                   give, take, send_i, recv_i, send_j, recv_j, send_l, recv_l, send_s, recv_s, send_g, recv_g,
                   send_up, send_down, send_k, recv_z):
    r, c = lax.axis_index("row"), lax.axis_index("col")
    z, k, chips = c // 2, c % 2, cols // 2
    share = part.shape[0] // rows
    halves = cols // rows
    relay = k == r % 2
    peers = [(r + i) % rows for i in range(1, rows)]
    col_peers = [(c + i) % cols for i in range(1, cols)]
    greet([(True, peer, c) for peer in peers] + [(True, r, peer) for peer in col_peers])

    def rows_of(q):
        return pl.ds(pl.multiple_of(q * share, share), share)

    def scatter(i):
        return remote(part.at[rows_of(peers[i - 1])], slots.at[i - 1], send_s.at[i - 1], recv_s.at[i - 1],
                      peers[i - 1], c)

    def gather(i):
        return remote(wct.at[rows_of(r)], wct.at[rows_of(r)], send_g.at[i - 1], recv_g.at[i - 1],
                      peers[i - 1], c)

    for i in range(1, rows):
        scatter(i).start()
    steps = coupling_steps(top, lower_inverse, coupling, shifted, work)
    steps.pop(0)()
    steps.pop(0)()
    total = part[rows_of(r), :]
    for i in range(1, rows):
        scatter(i).wait_recv()
        total = total + slots[i - 1]
    wct[rows_of(r), :] = total
    for i in range(1, rows):
        gather(i).start()

    size = share // cols
    term = dot_nt(total, vec_cols[...])
    for d in range(cols):
        give[d] = term[d * size:(d + 1) * size, :]

    def inner_scatter(i):
        return remote(give.at[col_peers[i - 1]], take.at[i - 1], send_i.at[i - 1], recv_i.at[i - 1],
                      r, col_peers[i - 1])

    def inner_gather(i):
        return remote(inner.at[r, c], inner.at[r, c], send_j.at[i - 1], recv_j.at[i - 1],
                      r, col_peers[i - 1])

    def inner_rows(i):
        return remote(inner.at[r], inner.at[r], send_l.at[i - 1], recv_l.at[i - 1], peers[i - 1], c)

    def inner_sum():
        piece = give[c]
        for i in range(1, cols):
            inner_scatter(i).wait_recv()
            piece = piece + take[i - 1]
        inner[r, c] = piece
        for i in range(1, cols):
            inner_gather(i).start()

    def inner_share():
        for i in range(1, cols):
            inner_gather(i).wait_recv()
        for i in range(1, rows):
            inner_rows(i).start()

    for i in range(1, cols):
        inner_scatter(i).start()
    steps.pop(0)()
    rounds = [inner_sum, inner_share]

    def origin(h):
        return (r + rows * h) // 2

    def piece(h, i):
        return wrt.at[h, rows_of((r + rows - i) % rows)]

    def up(h, i):
        return remote(piece(h, i), piece(h, i), send_up.at[h, i], recv_z.at[h, i], r, c + 2)

    def down(h, i):
        return remote(piece(h, i), piece(h, i), send_down.at[h, i], recv_z.at[h, i], r, c - 2)

    def across(h, i):
        return remote(piece(h, i), piece(h, i), send_k.at[h, i], recv_z.at[h, i], r, c + 1 - 2 * k)

    for i in range(rows):
        if i:
            gather(i).wait_recv()
        for h in range(halves):
            @pl.when(c == r + rows * h)
            def _(h=h, i=i):
                place = rows_of((r + rows - i) % rows)
                wrt[h, place, :] = wct[place, :]
                pl.when(z < chips - 1)(lambda: up(h, i).start())
                pl.when(z > 0)(lambda: down(h, i).start())
                across(h, i).start()

    for i in range(rows):
        for h in range(halves):
            @pl.when(c != r + rows * h)
            def _(h=h, i=i):
                across(h, i).wait_recv()

                @pl.when(relay)
                def _():
                    pl.when((z > origin(h)) & (z < chips - 1))(lambda: up(h, i).start())
                    pl.when((z < origin(h)) & (z > 0))(lambda: down(h, i).start())
                    across(h, i).start()
        if rounds:
            rounds.pop(0)()
        if steps:
            steps.pop(0)()

    for step_left in rounds + steps:
        step_left()

    for i in range(1, cols):
        inner_scatter(i).wait_send()
        inner_gather(i).wait_send()
    for i in range(1, rows):
        inner_rows(i).wait()

    for i in range(1, rows):
        scatter(i).wait_send()
        gather(i).wait_send()

    @pl.when(relay)
    def _():
        for i in range(rows):
            for h in range(halves):
                pl.when((z >= origin(h)) & (z < chips - 1))(lambda: up(h, i).wait_send())
                pl.when((z <= origin(h)) & (z > 0))(lambda: down(h, i).wait_send())
                across(h, i).wait_send()


def reduce_product(panel, rows, cols, part, top, lower_inverse, vec_cols):
    width, local_cols = part.shape
    halves, size = cols // rows, width // (rows * cols)
    dma = pltpu.SemaphoreType.DMA
    f32 = jnp.float32
    return pl.pallas_call(
        functools.partial(product_kernel, rows, cols),
        out_shape=(jax.ShapeDtypeStruct(part.shape, f32),
                   jax.ShapeDtypeStruct((halves, width, local_cols), f32),
                   jax.ShapeDtypeStruct((width, width), f32),
                   jax.ShapeDtypeStruct((rows, cols, size, width), f32)),
        in_specs=[VMEM] * 4,
        out_specs=(VMEM,) * 4,
        scratch_shapes=[pltpu.VMEM((rows - 1, width // rows, local_cols), f32),
                        pltpu.VMEM((width, 2 * width), f32), pltpu.VMEM((width, width), f32),
                        pltpu.VMEM((cols, size, width), f32), pltpu.VMEM((cols - 1, size, width), f32),
                        dma((cols - 1,)), dma((cols - 1,)), dma((cols - 1,)), dma((cols - 1,)),
                        dma((rows - 1,)), dma((rows - 1,)),
                        dma((rows - 1,)), dma((rows - 1,)), dma((rows - 1,)), dma((rows - 1,)),
                        dma((halves, rows)), dma((halves, rows)), dma((halves, rows)), dma((halves, rows))],
        compiler_params=pltpu.CompilerParams(collective_id=PANELS + panel, has_side_effects=True,
                                             vmem_limit_bytes=40 * 2**20),
        name=f"reduce_product_{panel}",
    )(part, top, lower_inverse, vec_cols)


def shards(matrix):
    row_blocks, width, col_blocks, _ = matrix.shape
    rows, cols = lax.axis_size("row"), lax.axis_size("col")
    halves = cols // rows
    row_index, col_index = lax.axis_index("row"), lax.axis_index("col")
    local_rows, local_cols = row_blocks * width, col_blocks * width
    dense = matrix.reshape(local_rows, local_cols)
    row_range = jnp.arange(local_rows, dtype=jnp.int32)
    col_range = jnp.arange(local_cols, dtype=jnp.int32)
    global_rows = (row_range // width * rows + row_index) * width + row_range % width
    global_cols = (col_range // width * cols + col_index) * width + col_range % width
    unit = jnp.arange(width, dtype=jnp.int32)
    for panel in range(PANELS):
        start = (panel + 1) * width
        col_slot, row_slot = panel // cols * width, panel // rows * width
        below = global_rows[:, None] >= start
        beside = global_cols[None, :] >= start
        low = jnp.where(below, dense[:, col_slot:col_slot + width], 0.0)
        right = jnp.where(beside, dense[row_slot:row_slot + width, :], 0.0)
        top_slot = (panel + 1) // rows * width
        xr, xct, gt, upper, lower_inverse = spread(panel, rows, cols, low, right, dot_tn(low, low),
                                                   low[top_slot:top_slot + width])
        placed_rows = (global_rows[:, None] - start == unit[None, :]).astype(jnp.float32)
        placed_cols = (global_cols[None, :] - start == unit[:, None]).astype(jnp.float32)
        vec_rows = dot_nt(xr, lower_inverse) + placed_rows
        vec_cols = dot(lower_inverse, xct) + placed_cols
        part = lax.dot_general(vec_rows, dense, (((0,), (0,)), ((), ())), precision=high,
                               preferred_element_type=jnp.float32)
        part = jnp.where(beside, part, 0.0)
        applied_cols, applied, coupling, inner = reduce_product(panel, rows, cols, part, gt[1],
                                                                lower_inverse, vec_cols)
        inner = inner.reshape(width, width)
        applied = applied.reshape(halves, width, col_blocks, width)
        applied_rows = applied.transpose(2, 0, 3, 1).reshape(local_rows, width)
        middle = dot_nt(dot(coupling, inner), coupling)
        factor_rows = dot_nt(applied_rows, coupling) - 0.5 * dot(vec_rows, middle)
        factor_cols = dot(coupling, applied_cols) - 0.5 * dot_tn(middle, vec_cols)
        dense = dense - dot(jnp.concatenate([factor_rows, vec_rows], axis=1),
                            jnp.concatenate([vec_cols, factor_cols], axis=0), high)
        old_col = dense[:, col_slot:col_slot + width]
        tiled = jnp.tile(-upper, (row_blocks, 1))
        on_top = (global_rows >= start) & (global_rows < start + width)
        new_col = jnp.where(below, jnp.where(on_top[:, None], tiled, 0.0), old_col)
        dense = dense.at[:, col_slot:col_slot + width].set(
            jnp.where(col_index == panel % cols, new_col, old_col))
        old_row = dense[row_slot:row_slot + width, :]
        tiled = jnp.tile(-upper.T, (1, col_blocks))
        on_top = (global_cols >= start) & (global_cols < start + width)
        new_row = jnp.where(beside, jnp.where(on_top[None, :], tiled, 0.0), old_row)
        dense = dense.at[row_slot:row_slot + width, :].set(
            jnp.where(row_index == panel % rows, new_row, old_row))
    return dense.reshape(matrix.shape)


def solution(mesh):
    assert mesh.shape["col"] % mesh.shape["row"] == 0 and mesh.shape["row"] % 2 == 0
    spec = P(None, "row", None, "col")
    return jax.shard_map(shards, mesh=mesh, in_specs=(spec,), out_specs=spec, check_vma=False)
```
